32 devices in a mesh: dp: 4 (over y, core), expert: 8 (over z, x).
Axes of the slice: x: 2, y: 2, z: 4, core: 2. Of those that a mesh axis runs over, the one named last changes fastest.
Arguments:
- qkv: bfloat16 [32, 128, 6144], P(('dp', 'expert')), may hold values from -6 to 6
- resid: bfloat16 [32, 128, 2048], P(('dp', 'expert')), may hold values from -54 to 54
- lengths: int32 [32], P(('dp', 'expert')), may hold values from 32 to 128
- norm_gain: float32 [2048], replicated, may hold values from 0.25 to 1.75
- expert_ids: int32 [32, 128, 2], P(('dp', 'expert')), may hold values from 0 to 7, all different within a row; in each aligned block of 128 rows (0 to 127, 128 to 255, ..., all dimensions but the last counted through in order) at most 64 rows name the same one
- gate_vals: bfloat16 [32, 128, 2], P(('dp', 'expert')), may hold values from 0.099609375 to 1
- w_gate: bfloat16 [8, 768, 2048], P('expert', None, 'dp'), may hold values from -0.125 to 0.125
- w_up: bfloat16 [8, 768, 2048], P('expert', None, 'dp'), may hold values from -0.125 to 0.125
- w_down: bfloat16 [8, 768, 2048], P('expert', None, 'dp'), may hold values from -0.21875 to 0.21875
- cotangent: bfloat16 [32, 128, 2048], P(('dp', 'expert')), may hold values from -6 to 6
Outputs:
- mixture: bfloat16 [32, 128, 2048], P(('dp', 'expert'))
- grad_stream: float32 [32, 128, 2048], P(('dp', 'expert'))
- grad_gate: float32 [8, 768, 2048], P('expert', None, 'dp')
- grad_up: float32 [8, 768, 2048], P('expert', None, 'dp')
- grad_down: float32 [8, 768, 2048], P('expert', None, 'dp')
The draws below stay inside these ranges and needn't reach their ends.
Inputs may be any that keep to these rules, and one draw needn't show every extreme that they name: `expert_ids`: among the 128 tokens of one device, no expert is named by more than 64 routes, a bound that some block reaches; the 2 ids of a token differ.
All inputs are finite; a program needn't handle non-finite values.
Results may differ from the reference program's by a relative error of at most 0.015.
Values may be sent and summed in bfloat16 or wider, within the bound.
A program may use at most 128 MiB of HBM per device.

```python
import math
import jax
import jax.numpy as jnp
import numpy as np
from jax import lax

D = 2048
HEADS = 16
HEAD = 128
FF = 768
TOP = 2
STEPS = 128
EXPERTS = 8
SERIES = 32
TOK_DEV = 128
GROUP = 8
CAP = 64
N_DP = 4
N_EXPERT = 8


def draw_qkv(key, part):
    first = jax.random.fold_in(key, 0)
    shape = (SERIES, STEPS, 3 * D)
    values = jnp.clip(jax.random.normal(first, shape, jnp.float32), -6.0, 6.0)
    return values.astype(jnp.bfloat16)


def draw_resid(key, part):
    first, second, third = jax.random.split(key, 3)
    shape = (SERIES, STEPS, D)
    columns = jnp.exp(jax.random.uniform(second, (D,), jnp.float32, math.log(0.3), math.log(3.0)))
    tokens = jnp.exp(jax.random.uniform(third, (SERIES, STEPS, 1), jnp.float32, math.log(0.3), math.log(3.0)))
    base = jnp.clip(jax.random.normal(first, shape, jnp.float32), -6.0, 6.0)
    return (base * columns * tokens).astype(jnp.bfloat16)


def draw_lengths(key, part):
    first, second = jax.random.split(key, 2)
    values = jax.random.randint(first, (SERIES,), STEPS // 4, STEPS + 1, jnp.int32)
    order = jax.random.permutation(second, SERIES)
    values = values.at[order[0]].set(STEPS).at[order[1]].set(STEPS // 4)
    return values.astype(jnp.int32)


def shard_levels(own_key, dims, pieces, low, top_value):
    level = 1.0
    for dim, blocks in pieces:
        heights = jax.random.uniform(jax.random.fold_in(jax.random.fold_in(own_key, 6), dim), (blocks,), jnp.float32, low / len(pieces), top_value / len(pieces))
        level = level * jnp.repeat(jnp.exp(heights), dims[dim] // blocks).reshape((-1,) + (1,) * (len(dims) - 1 - dim))
    return level


def routed_block(own_key, own, number, rows, amount, top, reach, slope):
    sequence = jax.random.permutation(own_key, amount)
    crowded, common = portions_of(amount, rows * top, reach, slope, True), portions_of(amount, rows * top, reach, slope, False)
    places = jnp.arange(amount)

    def named(sizes, rotation):
        used = int((sizes > 0).sum())
        fixed = max(1, used // 4)
        passed = fixed + (places - fixed + rotation * (used - fixed)) % max(1, amount - fixed)
        return jnp.zeros((amount,), jnp.int32).at[sequence[jnp.where(places < fixed, places, passed)]].set(jnp.asarray(sizes, jnp.int32))

    sizes = jnp.where(number % 4 == 0, named(crowded, number // 4), named(common, number - number // 4 - 1))
    mixed = jax.random.permutation(jax.random.fold_in(own, 3), amount)
    giver, sink = mixed[0:amount // 2 * 2:2], mixed[1:amount // 2 * 2:2]
    room = jnp.minimum(sizes[giver] - 1, reach - sizes[sink]) // 2
    room = jnp.where((giver == sequence[0]) | (sink == sequence[0]) | (sizes[sink] == 0), 0, jnp.maximum(room, 0))
    passed = jax.random.randint(jax.random.fold_in(own, 4), (amount // 2,), 0, 1 << 20) % (room + 1)
    sizes = sizes.at[giver].add(-passed).at[sink].add(passed)
    members = jnp.searchsorted(jnp.cumsum(sizes), jnp.arange(rows * top), side="right").astype(jnp.int32)
    listing = members.reshape(top, rows).T
    listing = listing[jax.random.permutation(jax.random.fold_in(own, 1), rows)]
    rotation = jax.random.randint(jax.random.fold_in(own, 2), (rows, 1), 0, top)
    return jnp.take_along_axis(listing, (jnp.arange(top)[None, :] + rotation) % top, axis=1)


def portions_of(amount, total, reach, lean, full):
    weights = [(1 << 20) // math.isqrt(standing ** lean) + 1 for standing in range(1, amount + 1)]
    largest = reach if full else min(reach, max(-(-total // amount), total * weights[0] // sum(weights)))
    least = 1 if total - largest >= amount - 1 else 0
    holding, rest = [largest] + [least] * (amount - 1), total - largest - least * (amount - 1)
    while rest > 0:
        candidates = [i for i in range(1, amount) if holding[i] < largest] or [i for i in range(1, amount) if holding[i] < reach]
        whole, remaining = sum([weights[i] for i in candidates]), rest
        for i in candidates:
            addition = min(reach - holding[i], max(1, remaining * weights[i] // whole), rest)
            holding[i] = holding[i] + addition
            rest = rest - addition
    return np.array(holding)


def scatter_about(own_key, extent, scale, limit, pieces=(), held_as=jnp.bfloat16):
    loudness = shard_levels(own_key, extent, pieces, -0.22, 0.18) if pieces else 1.0
    entries = jax.random.normal(own_key, extent, jnp.float32) * scale * loudness
    return jnp.minimum(jnp.maximum(entries, -limit), limit).astype(held_as)


def setup_inputs(seed: int = 0) -> dict:
    arg_keys = jax.random.split(jax.random.key(seed), 11)
    qkv = draw_qkv(jax.random.fold_in(arg_keys[10], 71), 0)
    resid = draw_resid(jax.random.fold_in(arg_keys[10], 71), 0)
    lengths = draw_lengths(jax.random.fold_in(arg_keys[10], 71), 0)
    norm_gain = jnp.clip(1.0 + 0.15 * jax.random.normal(arg_keys[3], (D,), jnp.float32), 0.25, 1.75)
    expert_ids_keys = jax.random.split(jax.random.fold_in(arg_keys[4], 1), SERIES * STEPS // TOK_DEV)
    expert_ids_turns = jax.random.permutation(jax.random.fold_in(arg_keys[4], 3), SERIES * STEPS // TOK_DEV)
    expert_ids = jax.vmap(lambda own, number: routed_block(jax.random.fold_in(arg_keys[4], 2), own, number, TOK_DEV, EXPERTS, TOP, CAP, 1))(expert_ids_keys, expert_ids_turns).reshape((SERIES, STEPS, TOP))
    gate_vals = jnp.clip(0.099609375 + 0.9003906 * jax.random.uniform(arg_keys[5], (SERIES, STEPS, TOP), jnp.float32) ** shard_levels(arg_keys[5], (SERIES, STEPS, TOP), ((0, 32),), -0.2, 0.2), 0.099609375, 1.0).astype(jnp.bfloat16)
    w_gate = scatter_about(arg_keys[6], (EXPERTS, FF, D), D ** -0.5, 0.125, ((0, 8), (2, 4)))
    w_up = scatter_about(arg_keys[7], (EXPERTS, FF, D), D ** -0.5, 0.125, ((0, 8), (2, 4)))
    w_down = scatter_about(arg_keys[8], (EXPERTS, FF, D), FF ** -0.5, 0.21875, ((0, 8), (2, 4)))
    cotangent = scatter_about(arg_keys[9], (SERIES, STEPS, D), 1.0, 6.0, ((0, 32),))
    return {"qkv": qkv, "resid": resid, "lengths": lengths, "norm_gain": norm_gain, "expert_ids": expert_ids, "gate_vals": gate_vals, "w_gate": w_gate, "w_up": w_up, "w_down": w_down, "cotangent": cotangent}


def attend(queries, key_rows, value_rows, live_mask):
    scores = jnp.einsum('sthc,uthc->thsu', queries.astype(jnp.float32), key_rows.astype(jnp.float32)) / math.sqrt(HEAD)
    count = queries.shape[0]
    self_pair = jnp.arange(count)[:, None] == jnp.arange(count)[None, :]
    allowed = jnp.transpose(live_mask)[:, None, None, :] | self_pair[None, None, :, :]
    masked = jnp.where(allowed, scores, -jnp.inf)
    highest = lax.optimization_barrier(jnp.max(masked, axis=-1, keepdims=True))
    raised = jnp.exp(masked - highest)
    weights = (raised / lax.optimization_barrier(jnp.sum(raised, axis=-1, keepdims=True))).astype(jnp.bfloat16)
    attended = jnp.einsum('thsu,uthc->sthc', weights.astype(jnp.float32), value_rows.astype(jnp.float32))
    attended = jnp.where(live_mask[:, :, None, None], attended, 0.0)
    return attended.astype(jnp.bfloat16)

def group_attend(inputs):
    packed, live_mask = inputs
    return attend(packed[:, :, 0], packed[:, :, 1], packed[:, :, 2], live_mask)

def expert_pass(inputs):
    x_rows, adjoint_rows, gate_rows, gate_weight, up_weight, down_weight = inputs
    gate_pre = jnp.dot(x_rows, gate_weight.T, preferred_element_type=jnp.float32)
    up_pre = jnp.dot(x_rows, up_weight.T, preferred_element_type=jnp.float32)
    sigmoid_gate = jax.nn.sigmoid(gate_pre)
    hidden = (gate_pre * sigmoid_gate * up_pre).astype(jnp.bfloat16)
    expert_out = jnp.dot(hidden, down_weight, preferred_element_type=jnp.float32).astype(jnp.bfloat16)
    grad_out = (gate_rows.astype(jnp.float32)[:, None] * adjoint_rows.astype(jnp.float32)).astype(jnp.bfloat16)
    grad_hidden = jnp.dot(grad_out, down_weight.T, preferred_element_type=jnp.float32)
    grad_gate_pre = (grad_hidden * up_pre * sigmoid_gate * (1.0 + gate_pre * (1.0 - sigmoid_gate))).astype(jnp.bfloat16)
    grad_up_pre = (grad_hidden * gate_pre * sigmoid_gate).astype(jnp.bfloat16)
    part_gate = jnp.dot(grad_gate_pre.T, x_rows, preferred_element_type=jnp.float32).astype(jnp.bfloat16)
    part_up = jnp.dot(grad_up_pre.T, x_rows, preferred_element_type=jnp.float32).astype(jnp.bfloat16)
    part_down = jnp.dot(hidden.T, grad_out, preferred_element_type=jnp.float32).astype(jnp.bfloat16)
    grad_rows = jnp.dot(grad_gate_pre, gate_weight, preferred_element_type=jnp.float32)
    grad_rows = (grad_rows + jnp.dot(grad_up_pre, up_weight, preferred_element_type=jnp.float32)).astype(jnp.bfloat16)
    return (expert_out, grad_rows, part_gate, part_up, part_down)

def reference(qkv, resid, lengths, norm_gain, expert_ids, gate_vals, w_gate, w_up, w_down, cotangent):
    packed = qkv.reshape(N_DP, GROUP, STEPS, 3, HEADS, HEAD)
    present = (jnp.arange(STEPS, dtype=jnp.int32)[None, :] < lengths[:, None]).reshape(N_DP, GROUP, STEPS)
    attended = lax.map(group_attend, (packed, present))
    stream = resid.astype(jnp.float32) + attended.reshape(SERIES, STEPS, D).astype(jnp.float32)
    inverse = 1.0 / jnp.sqrt(lax.optimization_barrier(jnp.mean(stream * stream, axis=-1, keepdims=True)) + 1e-05)
    normed = (stream * inverse * norm_gain).astype(jnp.bfloat16)
    block_count = N_DP * N_EXPERT
    per_block = TOK_DEV * TOP
    slot_count = N_EXPERT * CAP
    route_ids = expert_ids.reshape(block_count, per_block).astype(jnp.int32)
    onehot = (route_ids[:, :, None] == jnp.arange(EXPERTS, dtype=jnp.int32)[None, None, :]).astype(jnp.int32)
    running = jnp.cumsum(onehot, axis=1, dtype=jnp.int32) - 1
    position = lax.optimization_barrier(jnp.sum(running * onehot, axis=2, dtype=jnp.int32)).astype(jnp.int32)
    source = (jnp.arange(block_count, dtype=jnp.int32) % N_EXPERT)[:, None]
    slot_index = (route_ids * slot_count + source * CAP + position).astype(jnp.int32)
    group_tokens = GROUP * STEPS
    group_routes = group_tokens * TOP

    def group_pass(carry, inputs):
        normed_rows, adjoint_rows, gate_flat, index_flat = inputs
        filled = jnp.zeros((EXPERTS * slot_count,), jnp.int32).at[index_flat].set(jnp.arange(1, group_routes + 1, dtype=jnp.int32))
        token_of = jnp.where(filled > 0, (filled - 1) // TOP + 1, 0).astype(jnp.int32)
        normed_ext = jnp.concatenate([jnp.zeros((1, D), jnp.bfloat16), normed_rows], axis=0)
        adjoint_ext = jnp.concatenate([jnp.zeros((1, D), jnp.bfloat16), adjoint_rows], axis=0)
        gate_ext = jnp.concatenate([jnp.zeros((1,), jnp.bfloat16), gate_flat], axis=0)
        normed_buf = normed_ext[token_of].reshape(EXPERTS, slot_count, D)
        adjoint_buf = adjoint_ext[token_of].reshape(EXPERTS, slot_count, D)
        gate_buf = gate_ext[filled].reshape(EXPERTS, slot_count)
        out_buf, grad_buf, part_gate, part_up, part_down = lax.map(expert_pass, (normed_buf, adjoint_buf, gate_buf, w_gate, w_up, w_down))
        carry = (carry[0] + part_gate.astype(jnp.float32), carry[1] + part_up.astype(jnp.float32), carry[2] + part_down.astype(jnp.float32))
        out_route = out_buf.reshape(EXPERTS * slot_count, D)[index_flat].reshape(group_tokens, TOP, D)
        grad_route = grad_buf.reshape(EXPERTS * slot_count, D)[index_flat].reshape(group_tokens, TOP, D)
        gates = gate_flat.reshape(group_tokens, TOP).astype(jnp.float32)
        mixture = lax.optimization_barrier(jnp.sum(gates[:, :, None] * out_route.astype(jnp.float32), axis=1)).astype(jnp.bfloat16)
        grad_normed = lax.optimization_barrier(jnp.sum(grad_route.astype(jnp.float32), axis=1))
        return (carry, (mixture, grad_normed))
    empty = jnp.zeros((EXPERTS, FF, D), jnp.float32)
    inputs = (normed.reshape(N_DP, group_tokens, D), cotangent.reshape(N_DP, group_tokens, D), gate_vals.reshape(N_DP, group_routes), slot_index.reshape(N_DP, group_routes))
    grads, (mixture, grad_normed) = lax.scan(group_pass, (empty, empty, empty), inputs)
    mixture = mixture.reshape(SERIES, STEPS, D)
    grad_normed = grad_normed.reshape(SERIES, STEPS, D)
    scaled = norm_gain * grad_normed
    grad_stream = inverse * scaled - stream * inverse * inverse * inverse * lax.optimization_barrier(jnp.mean(stream * scaled, axis=-1, keepdims=True))
    return (mixture, grad_stream, grads[0], grads[1], grads[2])
```

```python
import functools
import math

import jax
import jax.numpy as jnp
from jax import lax
from jax.experimental import pallas as pl
from jax.experimental.pallas import tpu as pltpu
from jax.sharding import PartitionSpec as P

HEADS = 16
MESH = pl.DeviceIdType.MESH
F32 = jnp.float32
BF16 = jnp.bfloat16
NT = (((1,), (1,)), ((), ()))
NN = (((1,), (0,)), ((), ()))
LEN, QKV, ATT, COT, ROW, OUT, GRD = range(7)


def attend_block(queries, key_rows, value_rows, live_mask, head_size):
    scores = jnp.einsum(
        "sthc,uthc->thsu", queries, key_rows, preferred_element_type=jnp.float32
    ) / math.sqrt(head_size)
    count = queries.shape[0]
    self_pair = jnp.arange(count)[:, None] == jnp.arange(count)[None, :]
    allowed = jnp.transpose(live_mask)[:, None, None, :] | self_pair[None, None, :, :]
    masked = jnp.where(allowed, scores, -jnp.inf)
    highest = jnp.max(masked, axis=-1, keepdims=True)
    raised = jnp.exp(masked - highest)
    weights = (raised / jnp.sum(raised, axis=-1, keepdims=True)).astype(jnp.bfloat16)
    attended = jnp.einsum(
        "thsu,uthc->sthc", weights, value_rows, preferred_element_type=jnp.float32
    )
    attended = jnp.where(live_mask[:, :, None, None], attended, 0.0)
    return attended.astype(jnp.bfloat16)


def padded_rows(values):
    return jnp.concatenate([jnp.zeros((1,) + values.shape[1:], values.dtype), values], axis=0)


def plain_body(qkv, resid, lengths, norm_gain, expert_ids, gate_vals, w_gate, w_up, w_down, cotangent):
    series_here, step_count, triple = qkv.shape
    model_width = triple // 3
    head_size = model_width // HEADS
    experts_here = w_gate.shape[0]
    owners = lax.axis_size("expert")
    experts_all = experts_here * owners
    top_count = expert_ids.shape[2]
    tok_rows = series_here * step_count
    route_count = tok_rows * top_count
    capacity = 2 * route_count // experts_all
    slot_count = owners * capacity
    present = (jnp.arange(step_count)[None, :] < lengths[:, None]).astype(jnp.bfloat16)
    time_major, live_flags = (
        lax.all_to_all(qkv, "expert", split_axis=1, concat_axis=0, tiled=True),
        lax.all_to_all(present, "expert", split_axis=1, concat_axis=0, tiled=True),
    )
    group_size, time_count = live_flags.shape
    split_heads = time_major.reshape(group_size, time_count, 3, HEADS, head_size)
    attended = attend_block(
        split_heads[:, :, 0],
        split_heads[:, :, 1],
        split_heads[:, :, 2],
        live_flags > 0.5,
        head_size,
    )
    series_back = lax.all_to_all(
        attended.reshape(group_size, time_count, model_width),
        "expert",
        split_axis=0,
        concat_axis=1,
        tiled=True,
    )
    stream = resid.astype(jnp.float32) + series_back.astype(jnp.float32)
    inverse = 1.0 / jnp.sqrt(jnp.mean(stream * stream, axis=-1, keepdims=True) + 1e-05)
    normed = (stream * inverse * norm_gain).astype(jnp.bfloat16)
    route_ids = expert_ids.reshape(route_count)
    onehot = (route_ids[:, None] == jnp.arange(experts_all, dtype=jnp.int32)[None, :]).astype(
        jnp.int32
    )
    running = jnp.cumsum(onehot, axis=0, dtype=jnp.int32) - 1
    position = jnp.sum(running * onehot, axis=1, dtype=jnp.int32)
    slot_index = route_ids * capacity + position
    filled = (
        jnp.zeros((experts_all * capacity,), jnp.int32)
        .at[slot_index]
        .set(jnp.arange(1, route_count + 1, dtype=jnp.int32))
    )
    token_of = jnp.where(filled > 0, (filled - 1) // top_count + 1, 0)
    layout = (owners, experts_here, capacity, model_width)
    normed_send = padded_rows(normed.reshape(tok_rows, model_width))[token_of].reshape(layout)
    adjoint_send = padded_rows(cotangent.reshape(tok_rows, model_width))[token_of].reshape(layout)
    gate_send = padded_rows(gate_vals.reshape(route_count))[filled].reshape(
        owners, experts_here, capacity
    )
    gate_full, up_full, down_full = (
        lax.all_gather(w_gate, "dp", axis=2, tiled=True),
        lax.all_gather(w_up, "dp", axis=2, tiled=True),
        lax.all_gather(w_down, "dp", axis=2, tiled=True),
    )
    normed_recv = lax.all_to_all(normed_send, "expert", split_axis=0, concat_axis=2, tiled=True)
    x_rows = normed_recv.reshape(experts_here, slot_count, model_width)
    gate_pre = jnp.einsum("esd,efd->esf", x_rows, gate_full, preferred_element_type=jnp.float32)
    up_pre = jnp.einsum("esd,efd->esf", x_rows, up_full, preferred_element_type=jnp.float32)
    sigmoid_gate = jax.nn.sigmoid(gate_pre)
    hidden = (gate_pre * sigmoid_gate * up_pre).astype(jnp.bfloat16)
    expert_out = jnp.einsum(
        "esf,efd->esd", hidden, down_full, preferred_element_type=jnp.float32
    ).astype(jnp.bfloat16)
    back_shape = (1, experts_here, slot_count, model_width)
    out_home = lax.all_to_all(
        expert_out.reshape(back_shape), "expert", split_axis=2, concat_axis=0, tiled=True
    )
    adjoint_recv, gate_recv = (
        lax.all_to_all(adjoint_send, "expert", split_axis=0, concat_axis=2, tiled=True),
        lax.all_to_all(gate_send, "expert", split_axis=0, concat_axis=2, tiled=True),
    )
    adjoint_rows = adjoint_recv.reshape(experts_here, slot_count, model_width)
    gate_rows = gate_recv.reshape(experts_here, slot_count)
    grad_out = (
        gate_rows.astype(jnp.float32)[:, :, None] * adjoint_rows.astype(jnp.float32)
    ).astype(jnp.bfloat16)
    grad_hidden = jnp.einsum(
        "esd,efd->esf", grad_out, down_full, preferred_element_type=jnp.float32
    )
    grad_gate_pre = (
        grad_hidden * up_pre * sigmoid_gate * (1.0 + gate_pre * (1.0 - sigmoid_gate))
    ).astype(jnp.bfloat16)
    grad_up_pre = (grad_hidden * gate_pre * sigmoid_gate).astype(jnp.bfloat16)
    part_gate = jnp.einsum(
        "esf,esd->efd", grad_gate_pre, x_rows, preferred_element_type=jnp.float32
    )
    part_up = jnp.einsum("esf,esd->efd", grad_up_pre, x_rows, preferred_element_type=jnp.float32)
    part_down = jnp.einsum("esf,esd->efd", hidden, grad_out, preferred_element_type=jnp.float32)
    grad_gate, grad_up, grad_down = (
        lax.psum_scatter(
            part_gate.astype(jnp.bfloat16), "dp", scatter_dimension=2, tiled=True
        ).astype(jnp.float32),
        lax.psum_scatter(
            part_up.astype(jnp.bfloat16), "dp", scatter_dimension=2, tiled=True
        ).astype(jnp.float32),
        lax.psum_scatter(
            part_down.astype(jnp.bfloat16), "dp", scatter_dimension=2, tiled=True
        ).astype(jnp.float32),
    )
    grad_rows = jnp.einsum(
        "esf,efd->esd", grad_gate_pre, gate_full, preferred_element_type=jnp.float32
    )
    grad_rows = (
        grad_rows
        + jnp.einsum("esf,efd->esd", grad_up_pre, up_full, preferred_element_type=jnp.float32)
    ).astype(jnp.bfloat16)
    grad_home = lax.all_to_all(
        grad_rows.reshape(back_shape), "expert", split_axis=2, concat_axis=0, tiled=True
    )
    out_route = out_home.reshape(experts_all * capacity, model_width)[slot_index].reshape(
        tok_rows, top_count, model_width
    )
    grad_route = grad_home.reshape(experts_all * capacity, model_width)[slot_index].reshape(
        tok_rows, top_count, model_width
    )
    gates = gate_vals.reshape(tok_rows, top_count).astype(jnp.float32)
    mixture = jnp.sum(gates[:, :, None] * out_route.astype(jnp.float32), axis=1).astype(
        jnp.bfloat16
    )
    grad_normed = jnp.sum(grad_route.astype(jnp.float32), axis=1).reshape(
        series_here, step_count, model_width
    )
    scaled = norm_gain * grad_normed
    grad_stream = inverse * scaled - stream * inverse * inverse * inverse * jnp.mean(
        stream * scaled, axis=-1, keepdims=True
    )
    return (
        mixture.reshape(series_here, step_count, model_width),
        grad_stream,
        grad_gate,
        grad_up,
        grad_down,
    )


def dot(a, b, dims=NN):
    return lax.dot_general(a, b, dims, preferred_element_type=F32)


def layer_kernel(
    ne, nd, qkv, lens, resid, gain, meta, wg, wu, wd, cot,
    mixture, gstream, parts_in,
    len_in, qkv_in, att_out, att_in, normed, inv_rms, hit, hit_t, hit_gt,
    row_out, row_in, cot_out, cot_in, out_in, grd_in, w_all, gate, up, grad_h,
    hidden, hidden_t, ggp, ggp_t, gup, gup_t, parts_out,
    send, recv, w_send, w_recv, p_send, p_recv, local,
):
    me = lax.axis_index("expert")
    md = lax.axis_index("dp")
    steps, width = resid.shape
    ff, wcol = wg.shape
    tb = steps // ne
    slots = row_in.shape[0]
    cap = slots // ne
    head = width // HEADS

    def rows(block, size):
        return pl.ds(pl.multiple_of(block * size, size), size)

    def cols(block, size, base=0):
        return pl.ds(pl.multiple_of(base + block * size, 128), size)

    def remote(kind, src, dst, to, slot):
        return pltpu.make_async_remote_copy(
            src_ref=src, dst_ref=dst, send_sem=send.at[kind, to], recv_sem=recv.at[kind, slot],
            device_id={"expert": to}, device_id_type=MESH,
        )

    def ends(kind):
        if kind == LEN:
            return lens, len_in, None, tb
        if kind == QKV:
            return qkv, qkv_in, tb, tb
        if kind == ATT:
            return att_out, att_in, tb, tb
        if kind == COT:
            return cot_out, cot_in, cap, cap
        if kind == ROW:
            return row_out, row_in, cap, cap
        if kind == OUT:
            return row_out, out_in, cap, cap
        return cot_out, grd_in, cap, cap

    def copy_to(kind, to, slot):
        src, dst, from_rows, to_rows = ends(kind)
        part = src if from_rows is None else src.at[rows(to, from_rows)]
        return remote(kind, part, dst.at[rows(slot, to_rows)], to, slot)

    def own(kind):
        src, dst, from_rows, to_rows = ends(kind)
        part = src if from_rows is None else src.at[rows(me, from_rows)]
        return pltpu.make_async_copy(part, dst.at[rows(me, to_rows)], local.at[kind])

    def each(count, base, act):
        def step(i, carry):
            act(lax.rem(base + i, count))
            return carry

        lax.fori_loop(1, count, step, 0)

    def launch(kind):
        each(ne, me, lambda p: copy_to(kind, p, me).start())
        own(kind).start()

    def arrived(kind):
        each(ne, me, lambda p: copy_to(kind, p, p).wait_recv())
        own(kind).wait()

    def sent(kind):
        each(ne, me, lambda p: copy_to(kind, p, me).wait_send())

    shards = (wg, wu, wd)

    def weight_to(k, to, slot):
        return pltpu.make_async_remote_copy(
            src_ref=shards[k], dst_ref=w_all.at[k, slot], send_sem=w_send.at[k, to],
            recv_sem=w_recv.at[k, slot], device_id={"dp": to}, device_id_type=MESH,
        )

    def weight_own(k):
        return pltpu.make_async_copy(shards[k], w_all.at[k, md], local.at[7 + k])

    def part_to(k, to, slot):
        return pltpu.make_async_remote_copy(
            src_ref=parts_out.at[k, to], dst_ref=parts_in.at[k, slot], send_sem=p_send.at[k, to],
            recv_sem=p_recv.at[k, slot], device_id={"dp": to}, device_id_type=MESH,
        )

    def part_own(k):
        return pltpu.make_async_copy(parts_out.at[k, md], parts_in.at[k, md], local.at[10 + k])

    barrier = pltpu.get_barrier_semaphore()
    each(ne, me, lambda p: pl.semaphore_signal(
        barrier, inc=1, device_id={"expert": p}, device_id_type=MESH))
    each(nd, md, lambda p: pl.semaphore_signal(
        barrier, inc=1, device_id={"dp": p}, device_id_type=MESH))
    pl.semaphore_wait(barrier, ne + nd - 2)

    launch(LEN)
    launch(QKV)
    for k in range(3):
        each(nd, md, lambda p: weight_to(k, p, md).start())
        weight_own(k).start()

    top = max(16, ne)
    expert = lax.broadcasted_iota(jnp.int32, (top, steps), 0).astype(F32)
    first, second = meta[0:1, :], meta[1:2, :]
    named = jnp.where(expert == first, 1.0, 0.0) + jnp.where(expert == second, 1.0, 0.0)
    before = lax.broadcasted_iota(jnp.int32, (steps, steps), 0) < lax.broadcasted_iota(
        jnp.int32, (steps, steps), 1
    )
    place = dot(named.astype(BF16), jnp.where(before, 1.0, 0.0).astype(BF16))
    place = jnp.where(named > 0.5, place, -1.0)
    value = jnp.where(expert == first, meta[2:3, :], meta[3:4, :])
    slot = lax.broadcasted_iota(jnp.int32, (cap, steps), 0).astype(F32)
    per = max(1, 128 // cap)
    for e in range(0, ne, per):
        ones, weighted = [], []
        for i in range(e, e + per):
            same = place[i : i + 1, :] == slot
            ones.append(jnp.where(same, 1.0, 0.0))
            weighted.append(jnp.where(same, value[i : i + 1, :], 0.0))
        one = jnp.concatenate(ones, axis=0)
        scaled = jnp.concatenate(weighted, axis=0)
        span = slice(e * cap, (e + per) * cap)
        hit[span, :] = one.astype(BF16)
        hit_t[:, span] = one.T.astype(BF16)
        hit_gt[:, span] = scaled.T.astype(BF16)
        cot_out[span, :] = dot(scaled.astype(BF16), cot[...]).astype(BF16)

    arrived(LEN)
    arrived(QKV)
    row_len = len_in[...].astype(F32)
    col_len = row_len.T
    r_id = lax.broadcasted_iota(jnp.int32, (steps, steps), 0)
    c_id = lax.broadcasted_iota(jnp.int32, (steps, steps), 1)
    r_time, c_time = lax.rem(r_id, tb), lax.rem(c_id, tb)
    start = me * tb
    seen = ((c_time + start).astype(F32) < col_len) | (r_id == c_id)
    bias = jnp.where((r_time == c_time) & seen, 0.0, -jnp.inf)
    live = jnp.where((r_time + start).astype(F32) < row_len, 1.0, 0.0)

    def attend(h, carry):
        q = qkv_in[:, cols(h, head)]
        k = qkv_in[:, cols(h, head, width)]
        v = qkv_in[:, cols(h, head, 2 * width)]
        scores = dot(q, k, NT) / math.sqrt(head) + bias
        raised = jnp.exp(scores - jnp.max(scores, axis=1, keepdims=True))
        weights = (raised / jnp.sum(raised, axis=1, keepdims=True)).astype(BF16)
        att_out[:, cols(h, head)] = (dot(weights, v) * live).astype(BF16)
        return carry

    lax.fori_loop(0, HEADS, attend, 0)
    launch(ATT)
    launch(COT)
    arrived(ATT)

    def norm(i, carry):
        r = rows(i, 16)
        stream = resid[r, :].astype(F32) + att_in[r, :].astype(F32)
        mean = jnp.sum(stream * stream, axis=1, keepdims=True) / width
        inverse = 1.0 / jnp.sqrt(mean + 1e-05)
        inv_rms[r, :] = jnp.broadcast_to(inverse, (16, 128))
        normed[r, :] = (stream * inverse * gain[...]).astype(BF16)
        return carry

    lax.fori_loop(0, steps // 16, norm, 0)

    def dispatch(j, carry):
        c = cols(j, wcol)
        row_out[:, c] = dot(hit[...], normed[:, c]).astype(BF16)
        return carry

    lax.fori_loop(0, nd, dispatch, 0)
    launch(ROW)
    for k in range(3):
        each(nd, md, lambda p: weight_to(k, p, p).wait_recv())
        weight_own(k).wait()
    arrived(ROW)

    gate[...] = jnp.zeros_like(gate)
    up[...] = jnp.zeros_like(up)
    grad_h[...] = jnp.zeros_like(grad_h)

    def forward(j, carry):
        x = row_in[:, cols(j, wcol)]
        gate[...] += dot(x, w_all[0, j], NT)
        up[...] += dot(x, w_all[1, j], NT)
        return carry

    lax.fori_loop(0, nd, forward, 0)

    def activate(i, carry):
        r = rows(i, 128)
        g = gate[r, :]
        value = g * (1.0 / (1.0 + jnp.exp(-g))) * up[r, :]
        hidden[r, :] = value.astype(BF16)
        hidden_t[:, cols(i, 128)] = value.T.astype(BF16)
        return carry

    lax.fori_loop(0, slots // 128, activate, 0)
    sent(ROW)

    def project(j, carry):
        row_out[:, cols(j, wcol)] = dot(hidden[...], w_all[2, j]).astype(BF16)
        return carry

    lax.fori_loop(0, nd, project, 0)
    launch(OUT)

    arrived(COT)

    def backward(j, carry):
        grad_h[...] += dot(cot_in[:, cols(j, wcol)], w_all[2, j], NT)
        return carry

    lax.fori_loop(0, nd, backward, 0)

    def differentiate(i, carry):
        r = rows(i, 128)
        c = cols(i, 128)
        g = gate[r, :]
        gh = grad_h[r, :]
        s = 1.0 / (1.0 + jnp.exp(-g))
        dg = gh * up[r, :] * s * (1.0 + g * (1.0 - s))
        ggp[r, :] = dg.astype(BF16)
        ggp_t[:, c] = dg.T.astype(BF16)
        du = gh * g * s
        gup[r, :] = du.astype(BF16)
        gup_t[:, c] = du.T.astype(BF16)
        return carry

    lax.fori_loop(0, slots // 128, differentiate, 0)

    def weigh(j):
        x = row_in[:, cols(j, wcol)]
        y = cot_in[:, cols(j, wcol)]
        parts_out[0, j] = dot(ggp_t[...], x).astype(BF16)
        parts_out[1, j] = dot(gup_t[...], x).astype(BF16)
        parts_out[2, j] = dot(hidden_t[...], y).astype(BF16)

    def weigh_send(j):
        weigh(j)
        for k in range(3):
            part_to(k, j, md).start()

    each(nd, md, weigh_send)
    sent(COT)

    def pull(j, carry):
        c = cols(j, wcol)
        cot_out[:, c] = (dot(ggp[...], w_all[0, j]) + dot(gup[...], w_all[1, j])).astype(BF16)
        return carry

    lax.fori_loop(0, nd, pull, 0)
    launch(GRD)
    weigh(md)
    for k in range(3):
        part_own(k).start()

    arrived(OUT)

    def mix(j, carry):
        c = cols(j, wcol)
        mixture[:, c] = dot(hit_gt[...], out_in[:, c]).astype(BF16)
        return carry

    lax.fori_loop(0, nd, mix, 0)
    arrived(GRD)

    def home(j, carry):
        c = cols(j, wcol)
        gstream[:, c] = dot(hit_t[...], grd_in[:, c])
        return carry

    lax.fori_loop(0, nd, home, 0)

    def finish(i, carry):
        r = rows(i, 16)
        stream = resid[r, :].astype(F32) + att_in[r, :].astype(F32)
        inverse = inv_rms[r, 0:1]
        scaled = gain[...] * gstream[r, :]
        mean = jnp.sum(stream * scaled, axis=1, keepdims=True) / width
        gstream[r, :] = inverse * scaled - stream * (inverse * inverse * inverse * mean)
        return carry

    lax.fori_loop(0, steps // 16, finish, 0)

    for k in range(3):
        each(nd, md, lambda p: part_to(k, p, p).wait_recv())
        each(nd, md, lambda p: part_to(k, p, md).wait_send())
        part_own(k).wait()
        each(nd, md, lambda p: weight_to(k, p, md).wait_send())
    for kind in (LEN, QKV, ATT, OUT, GRD):
        sent(kind)


def body(qkv, resid, lengths, norm_gain, expert_ids, gate_vals, w_gate, w_up, w_down, cotangent):
    series, steps, triple = qkv.shape
    width = triple // 3
    ne, nd = lax.axis_size("expert"), lax.axis_size("dp")
    _, ff, wcol = w_gate.shape
    routes = steps * expert_ids.shape[2]
    cap = 2 * routes // ne
    slots = ne * cap
    tb = steps // ne
    fits = (
        series == 1 and w_gate.shape[0] == 1 and steps == 128 and tb % 16 == 0
        and cap % 16 == 0 and slots % 128 == 0 and wcol % 128 == 0 and expert_ids.shape[2] == 2
        and width // HEADS == 128
    )
    if not fits:
        return plain_body(
            qkv, resid, lengths, norm_gain, expert_ids, gate_vals, w_gate, w_up, w_down, cotangent
        )
    meta = jnp.concatenate([expert_ids[0].astype(F32), gate_vals[0].astype(F32)], axis=1).T
    lens = jnp.broadcast_to(lengths.astype(BF16)[:, None], (tb, 128))
    vmem = pl.BlockSpec(memory_space=pltpu.VMEM)
    hbm = pl.BlockSpec(memory_space=pl.ANY)
    dma = pltpu.SemaphoreType.DMA
    flops = 2 * slots * ff * width * 9
    mixture, gstream, parts = pl.pallas_call(
        functools.partial(layer_kernel, ne, nd),
        out_shape=(
            jax.ShapeDtypeStruct((steps, width), BF16),
            jax.ShapeDtypeStruct((steps, width), F32),
            jax.ShapeDtypeStruct((3, nd, ff, wcol), BF16),
        ),
        in_specs=[hbm, vmem, vmem, vmem, vmem, hbm, hbm, hbm, vmem],
        out_specs=(vmem, vmem, hbm),
        scratch_shapes=[
            pltpu.VMEM((ne * tb, 128), BF16),
            pltpu.VMEM((steps, triple), BF16),
            pltpu.VMEM((steps, width), BF16),
            pltpu.VMEM((steps, width), BF16),
            pltpu.VMEM((steps, width), BF16),
            pltpu.VMEM((steps, 128), F32),
            pltpu.VMEM((slots, steps), BF16),
            pltpu.VMEM((steps, slots), BF16),
            pltpu.VMEM((steps, slots), BF16),
            pltpu.VMEM((slots, width), BF16),
            pltpu.VMEM((slots, width), BF16),
            pltpu.VMEM((slots, width), BF16),
            pltpu.VMEM((slots, width), BF16),
            pltpu.VMEM((slots, width), BF16),
            pltpu.VMEM((slots, width), BF16),
            pltpu.VMEM((3, nd, ff, wcol), BF16),
            pltpu.VMEM((slots, ff), F32),
            pltpu.VMEM((slots, ff), F32),
            pltpu.VMEM((slots, ff), F32),
            pltpu.VMEM((slots, ff), BF16),
            pltpu.VMEM((ff, slots), BF16),
            pltpu.VMEM((slots, ff), BF16),
            pltpu.VMEM((ff, slots), BF16),
            pltpu.VMEM((slots, ff), BF16),
            pltpu.VMEM((ff, slots), BF16),
            pltpu.VMEM((3, nd, ff, wcol), BF16),
            dma((7, ne)),
            dma((7, ne)),
            dma((3, nd)),
            dma((3, nd)),
            dma((3, nd)),
            dma((3, nd)),
            dma((16,)),
        ],
        compiler_params=pltpu.CompilerParams(
            collective_id=0, has_side_effects=True, vmem_limit_bytes=60 * 1024 * 1024
        ),
        cost_estimate=pl.CostEstimate(
            flops=flops, bytes_accessed=30_000_000, transcendentals=2 * slots * ff
        ),
    )(
        qkv[0], lens, resid[0], norm_gain[None, :], meta, w_gate[0], w_up[0], w_down[0],
        cotangent[0],
    )
    grads = [jnp.sum(parts[k].astype(F32), axis=0)[None] for k in range(3)]
    return (mixture[None], gstream[None], *grads)


def solution(mesh):
    in_specs = (
        P(("dp", "expert"), None, None),
        P(("dp", "expert"), None, None),
        P(("dp", "expert")),
        P(),
        P(("dp", "expert"), None, None),
        P(("dp", "expert"), None, None),
        P("expert", None, "dp"),
        P("expert", None, "dp"),
        P("expert", None, "dp"),
        P(("dp", "expert"), None, None),
    )
    out_specs = (
        P(("dp", "expert"), None, None),
        P(("dp", "expert"), None, None),
        P("expert", None, "dp"),
        P("expert", None, "dp"),
        P("expert", None, "dp"),
    )
    return jax.shard_map(body, mesh=mesh, in_specs=in_specs, out_specs=out_specs, check_vma=False)
```

```python
import functools
import math

import jax
import jax.numpy as jnp
from jax import lax
from jax.experimental import pallas as pl
from jax.experimental.pallas import tpu as pltpu
from jax.sharding import PartitionSpec as P

HEADS = 16
MESH = pl.DeviceIdType.MESH
F32 = jnp.float32
BF16 = jnp.bfloat16
NT = (((1,), (1,)), ((), ()))
NN = (((1,), (0,)), ((), ()))
LEN, QKV, ATT, COT, ROW, OUT, GRD, COT2 = range(8)


def attend_block(queries, key_rows, value_rows, live_mask, head_size):
    scores = jnp.einsum(
        "sthc,uthc->thsu", queries, key_rows, preferred_element_type=jnp.float32
    ) / math.sqrt(head_size)
    count = queries.shape[0]
    self_pair = jnp.arange(count)[:, None] == jnp.arange(count)[None, :]
    allowed = jnp.transpose(live_mask)[:, None, None, :] | self_pair[None, None, :, :]
    masked = jnp.where(allowed, scores, -jnp.inf)
    highest = jnp.max(masked, axis=-1, keepdims=True)
    raised = jnp.exp(masked - highest)
    weights = (raised / jnp.sum(raised, axis=-1, keepdims=True)).astype(jnp.bfloat16)
    attended = jnp.einsum(
        "thsu,uthc->sthc", weights, value_rows, preferred_element_type=jnp.float32
    )
    attended = jnp.where(live_mask[:, :, None, None], attended, 0.0)
    return attended.astype(jnp.bfloat16)


def padded_rows(values):
    return jnp.concatenate([jnp.zeros((1,) + values.shape[1:], values.dtype), values], axis=0)


def plain_body(qkv, resid, lengths, norm_gain, expert_ids, gate_vals, w_gate, w_up, w_down, cotangent):
    series_here, step_count, triple = qkv.shape
    model_width = triple // 3
    head_size = model_width // HEADS
    experts_here = w_gate.shape[0]
    owners = lax.axis_size("expert")
    experts_all = experts_here * owners
    top_count = expert_ids.shape[2]
    tok_rows = series_here * step_count
    route_count = tok_rows * top_count
    capacity = 2 * route_count // experts_all
    slot_count = owners * capacity
    present = (jnp.arange(step_count)[None, :] < lengths[:, None]).astype(jnp.bfloat16)
    time_major, live_flags = (
        lax.all_to_all(qkv, "expert", split_axis=1, concat_axis=0, tiled=True),
        lax.all_to_all(present, "expert", split_axis=1, concat_axis=0, tiled=True),
    )
    group_size, time_count = live_flags.shape
    split_heads = time_major.reshape(group_size, time_count, 3, HEADS, head_size)
    attended = attend_block(
        split_heads[:, :, 0],
        split_heads[:, :, 1],
        split_heads[:, :, 2],
        live_flags > 0.5,
        head_size,
    )
    series_back = lax.all_to_all(
        attended.reshape(group_size, time_count, model_width),
        "expert",
        split_axis=0,
        concat_axis=1,
        tiled=True,
    )
    stream = resid.astype(jnp.float32) + series_back.astype(jnp.float32)
    inverse = 1.0 / jnp.sqrt(jnp.mean(stream * stream, axis=-1, keepdims=True) + 1e-05)
    normed = (stream * inverse * norm_gain).astype(jnp.bfloat16)
    route_ids = expert_ids.reshape(route_count)
    onehot = (route_ids[:, None] == jnp.arange(experts_all, dtype=jnp.int32)[None, :]).astype(
        jnp.int32
    )
    running = jnp.cumsum(onehot, axis=0, dtype=jnp.int32) - 1
    position = jnp.sum(running * onehot, axis=1, dtype=jnp.int32)
    slot_index = route_ids * capacity + position
    filled = (
        jnp.zeros((experts_all * capacity,), jnp.int32)
        .at[slot_index]
        .set(jnp.arange(1, route_count + 1, dtype=jnp.int32))
    )
    token_of = jnp.where(filled > 0, (filled - 1) // top_count + 1, 0)
    layout = (owners, experts_here, capacity, model_width)
    normed_send = padded_rows(normed.reshape(tok_rows, model_width))[token_of].reshape(layout)
    adjoint_send = padded_rows(cotangent.reshape(tok_rows, model_width))[token_of].reshape(layout)
    gate_send = padded_rows(gate_vals.reshape(route_count))[filled].reshape(
        owners, experts_here, capacity
    )
    gate_full, up_full, down_full = (
        lax.all_gather(w_gate, "dp", axis=2, tiled=True),
        lax.all_gather(w_up, "dp", axis=2, tiled=True),
        lax.all_gather(w_down, "dp", axis=2, tiled=True),
    )
    normed_recv = lax.all_to_all(normed_send, "expert", split_axis=0, concat_axis=2, tiled=True)
    x_rows = normed_recv.reshape(experts_here, slot_count, model_width)
    gate_pre = jnp.einsum("esd,efd->esf", x_rows, gate_full, preferred_element_type=jnp.float32)
    up_pre = jnp.einsum("esd,efd->esf", x_rows, up_full, preferred_element_type=jnp.float32)
    sigmoid_gate = jax.nn.sigmoid(gate_pre)
    hidden = (gate_pre * sigmoid_gate * up_pre).astype(jnp.bfloat16)
    expert_out = jnp.einsum(
        "esf,efd->esd", hidden, down_full, preferred_element_type=jnp.float32
    ).astype(jnp.bfloat16)
    back_shape = (1, experts_here, slot_count, model_width)
    out_home = lax.all_to_all(
        expert_out.reshape(back_shape), "expert", split_axis=2, concat_axis=0, tiled=True
    )
    adjoint_recv, gate_recv = (
        lax.all_to_all(adjoint_send, "expert", split_axis=0, concat_axis=2, tiled=True),
        lax.all_to_all(gate_send, "expert", split_axis=0, concat_axis=2, tiled=True),
    )
    adjoint_rows = adjoint_recv.reshape(experts_here, slot_count, model_width)
    gate_rows = gate_recv.reshape(experts_here, slot_count)
    grad_out = (
        gate_rows.astype(jnp.float32)[:, :, None] * adjoint_rows.astype(jnp.float32)
    ).astype(jnp.bfloat16)
    grad_hidden = jnp.einsum(
        "esd,efd->esf", grad_out, down_full, preferred_element_type=jnp.float32
    )
    grad_gate_pre = (
        grad_hidden * up_pre * sigmoid_gate * (1.0 + gate_pre * (1.0 - sigmoid_gate))
    ).astype(jnp.bfloat16)
    grad_up_pre = (grad_hidden * gate_pre * sigmoid_gate).astype(jnp.bfloat16)
    part_gate = jnp.einsum(
        "esf,esd->efd", grad_gate_pre, x_rows, preferred_element_type=jnp.float32
    )
    part_up = jnp.einsum("esf,esd->efd", grad_up_pre, x_rows, preferred_element_type=jnp.float32)
    part_down = jnp.einsum("esf,esd->efd", hidden, grad_out, preferred_element_type=jnp.float32)
    grad_gate, grad_up, grad_down = (
        lax.psum_scatter(
            part_gate.astype(jnp.bfloat16), "dp", scatter_dimension=2, tiled=True
        ).astype(jnp.float32),
        lax.psum_scatter(
            part_up.astype(jnp.bfloat16), "dp", scatter_dimension=2, tiled=True
        ).astype(jnp.float32),
        lax.psum_scatter(
            part_down.astype(jnp.bfloat16), "dp", scatter_dimension=2, tiled=True
        ).astype(jnp.float32),
    )
    grad_rows = jnp.einsum(
        "esf,efd->esd", grad_gate_pre, gate_full, preferred_element_type=jnp.float32
    )
    grad_rows = (
        grad_rows
        + jnp.einsum("esf,efd->esd", grad_up_pre, up_full, preferred_element_type=jnp.float32)
    ).astype(jnp.bfloat16)
    grad_home = lax.all_to_all(
        grad_rows.reshape(back_shape), "expert", split_axis=2, concat_axis=0, tiled=True
    )
    out_route = out_home.reshape(experts_all * capacity, model_width)[slot_index].reshape(
        tok_rows, top_count, model_width
    )
    grad_route = grad_home.reshape(experts_all * capacity, model_width)[slot_index].reshape(
        tok_rows, top_count, model_width
    )
    gates = gate_vals.reshape(tok_rows, top_count).astype(jnp.float32)
    mixture = jnp.sum(gates[:, :, None] * out_route.astype(jnp.float32), axis=1).astype(
        jnp.bfloat16
    )
    grad_normed = jnp.sum(grad_route.astype(jnp.float32), axis=1).reshape(
        series_here, step_count, model_width
    )
    scaled = norm_gain * grad_normed
    grad_stream = inverse * scaled - stream * inverse * inverse * inverse * jnp.mean(
        stream * scaled, axis=-1, keepdims=True
    )
    return (
        mixture.reshape(series_here, step_count, model_width),
        grad_stream,
        grad_gate,
        grad_up,
        grad_down,
    )


def dot(a, b, dims=NN):
    return lax.dot_general(a, b, dims, preferred_element_type=F32)


def layer_kernel(
    ne, nd, qkv, lens, resid, gain, meta, wg, wu, wd, cot,
    mixture, gstream, g_gate, g_up, g_down,
    len_in, qkv_in, att_out, att_in, normed, inv_rms, hit, hit_t, hit_gt,
    row_out, row_in, cot_out, cot_in, out_in, grd_in, w_all, gate, up, grad_h,
    hidden, hidden_t, ggp, ggp_t, gup, gup_t,
    sib_out, sib_in, kept, far_in, total,
    send, recv, w_send, w_recv, s_send, s_recv, f_send, f_recv, local,
):
    me = lax.axis_index("expert")
    md = lax.axis_index("dp")
    steps, width = resid.shape
    ff, wcol = wg.shape
    sib = md + 1 - 2 * lax.rem(md, 2)
    far = lax.rem(md + 2, nd)
    diag = lax.rem(sib + 2, nd)
    tb = steps // ne
    slots = row_in.shape[0]
    cap = slots // ne
    head = width // HEADS

    def rows(block, size):
        return pl.ds(pl.multiple_of(block * size, size), size)

    def cols(block, size, base=0):
        return pl.ds(pl.multiple_of(base + block * size, 128), size)

    def remote(kind, src, dst, to, slot):
        return pltpu.make_async_remote_copy(
            src_ref=src, dst_ref=dst, send_sem=send.at[kind, to], recv_sem=recv.at[kind, slot],
            device_id={"expert": to}, device_id_type=MESH,
        )

    def ends(kind):
        if kind == LEN:
            return lens, len_in, None, tb
        if kind == QKV:
            return qkv, qkv_in, tb, tb
        if kind == ATT:
            return att_out, att_in, tb, tb
        if kind in (COT, COT2):
            return cot_out, cot_in, cap, cap
        if kind == ROW:
            return row_out, row_in, cap, cap
        if kind == OUT:
            return row_out, out_in, cap, cap
        return cot_out, grd_in, cap, cap

    def span(kind, block, size):
        if kind == COT:
            return rows(2 * block, size // 2)
        if kind == COT2:
            return rows(2 * block + 1, size // 2)
        return rows(block, size)

    def copy_to(kind, to, slot):
        src, dst, from_rows, to_rows = ends(kind)
        part = src if from_rows is None else src.at[span(kind, to, from_rows)]
        return remote(kind, part, dst.at[span(kind, slot, to_rows)], to, slot)

    def own(kind):
        src, dst, from_rows, to_rows = ends(kind)
        part = src if from_rows is None else src.at[span(kind, me, from_rows)]
        return pltpu.make_async_copy(part, dst.at[span(kind, me, to_rows)], local.at[kind])

    def each(count, base, act):
        def step(i, carry):
            act(lax.rem(base + i, count))
            return carry

        lax.fori_loop(1, count, step, 0)

    def launch(kind):
        each(ne, me, lambda p: copy_to(kind, p, me).start())
        own(kind).start()

    def arrived(kind):
        each(ne, me, lambda p: copy_to(kind, p, p).wait_recv())
        own(kind).wait()

    def sent(kind):
        each(ne, me, lambda p: copy_to(kind, p, me).wait_send())

    shards = (wg, wu, wd)

    def weight_to(k, way, slot):
        src = w_all.at[k, slot] if way == 2 else shards[k]
        return pltpu.make_async_remote_copy(
            src_ref=src, dst_ref=w_all.at[k, slot], send_sem=w_send.at[k, way],
            recv_sem=w_recv.at[k, slot], device_id={"dp": far if way == 1 else sib},
            device_id_type=MESH,
        )

    def weight_own(k):
        return pltpu.make_async_copy(shards[k], w_all.at[k, md], local.at[8 + k])

    def near_part(k, half):
        return pltpu.make_async_remote_copy(
            src_ref=sib_out.at[k, half], dst_ref=sib_in.at[k, half], send_sem=s_send.at[k, half],
            recv_sem=s_recv.at[k, half], device_id={"dp": sib}, device_id_type=MESH,
        )

    def far_part(k):
        return pltpu.make_async_remote_copy(
            src_ref=kept.at[k, 0], dst_ref=far_in.at[k], send_sem=f_send.at[k],
            recv_sem=f_recv.at[k], device_id={"dp": far}, device_id_type=MESH,
        )

    def result(k):
        return pltpu.make_async_copy(total.at[k], (g_gate, g_up, g_down)[k], local.at[11 + k])

    barrier = pltpu.get_barrier_semaphore()
    each(ne, me, lambda p: pl.semaphore_signal(
        barrier, inc=1, device_id={"expert": p}, device_id_type=MESH))
    for p in (sib, far):
        pl.semaphore_signal(barrier, inc=1, device_id={"dp": p}, device_id_type=MESH)
    pl.semaphore_wait(barrier, ne + 1)

    launch(LEN)
    launch(QKV)
    for k in range(3):
        weight_to(k, 1, md).start()
        weight_to(k, 0, md).start()
        weight_own(k).start()

    top = max(16, ne)
    expert = lax.broadcasted_iota(jnp.int32, (top, steps), 0).astype(F32)
    first, second = meta[0:1, :], meta[1:2, :]
    named = jnp.where(expert == first, 1.0, 0.0) + jnp.where(expert == second, 1.0, 0.0)
    before = lax.broadcasted_iota(jnp.int32, (steps, steps), 0) < lax.broadcasted_iota(
        jnp.int32, (steps, steps), 1
    )
    place = dot(named.astype(BF16), jnp.where(before, 1.0, 0.0).astype(BF16))
    place = jnp.where(named > 0.5, place, -1.0)
    value = jnp.where(expert == first, meta[2:3, :], meta[3:4, :])
    slot = lax.broadcasted_iota(jnp.int32, (cap, steps), 0).astype(F32)
    per = max(1, 128 // cap)
    for e in range(0, ne, per):
        ones, weighted = [], []
        for i in range(e, e + per):
            same = place[i : i + 1, :] == slot
            ones.append(jnp.where(same, 1.0, 0.0))
            weighted.append(jnp.where(same, value[i : i + 1, :], 0.0))
        one = jnp.concatenate(ones, axis=0)
        scaled = jnp.concatenate(weighted, axis=0)
        piece = slice(e * cap, (e + per) * cap)
        hit[piece, :] = one.astype(BF16)
        hit_t[:, piece] = one.T.astype(BF16)
        hit_gt[:, piece] = scaled.T.astype(BF16)
        cot_out[piece, :] = dot(scaled.astype(BF16), cot[...]).astype(BF16)

    arrived(LEN)
    arrived(QKV)
    launch(COT)
    row_len = len_in[...].astype(F32)
    col_len = row_len.T
    r_id = lax.broadcasted_iota(jnp.int32, (steps, steps), 0)
    c_id = lax.broadcasted_iota(jnp.int32, (steps, steps), 1)
    r_time, c_time = lax.rem(r_id, tb), lax.rem(c_id, tb)
    start = me * tb
    seen = ((c_time + start).astype(F32) < col_len) | (r_id == c_id)
    bias = jnp.where((r_time == c_time) & seen, 0.0, -jnp.inf)
    live = jnp.where((r_time + start).astype(F32) < row_len, 1.0, 0.0)

    def attend(h, carry):
        q = qkv_in[:, cols(h, head)]
        k = qkv_in[:, cols(h, head, width)]
        v = qkv_in[:, cols(h, head, 2 * width)]
        scores = dot(q, k, NT) / math.sqrt(head) + bias
        raised = jnp.exp(scores - jnp.max(scores, axis=1, keepdims=True))
        weights = (raised / jnp.sum(raised, axis=1, keepdims=True)).astype(BF16)
        att_out[:, cols(h, head)] = (dot(weights, v) * live).astype(BF16)
        return carry

    lax.fori_loop(0, HEADS, attend, 0)
    launch(ATT)
    arrived(ATT)

    def norm(i, carry):
        r = rows(i, 16)
        stream = resid[r, :].astype(F32) + att_in[r, :].astype(F32)
        mean = jnp.sum(stream * stream, axis=1, keepdims=True) / width
        inverse = 1.0 / jnp.sqrt(mean + 1e-05)
        inv_rms[r, :] = jnp.broadcast_to(inverse, (16, 128))
        normed[r, :] = (stream * inverse * gain[...]).astype(BF16)
        return carry

    lax.fori_loop(0, steps // 16, norm, 0)

    def dispatch(j, carry):
        c = cols(j, wcol)
        row_out[:, c] = dot(hit[...], normed[:, c]).astype(BF16)
        return carry

    lax.fori_loop(0, nd, dispatch, 0)
    launch(ROW)
    for k in range(3):
        weight_to(k, 1, far).wait_recv()
        weight_to(k, 2, far).start()
    sent(ROW)
    launch(COT2)
    for k in range(3):
        weight_to(k, 0, sib).wait_recv()
        weight_to(k, 2, diag).wait_recv()
        weight_own(k).wait()
    arrived(ROW)

    gate[...] = jnp.zeros_like(gate)
    up[...] = jnp.zeros_like(up)
    grad_h[...] = jnp.zeros_like(grad_h)

    def forward(j, carry):
        x = row_in[:, cols(j, wcol)]
        gate[...] += dot(x, w_all[0, j], NT)
        up[...] += dot(x, w_all[1, j], NT)
        return carry

    lax.fori_loop(0, nd, forward, 0)

    def activate(i, carry):
        r = rows(i, 128)
        g = gate[r, :]
        value = g * (1.0 / (1.0 + jnp.exp(-g))) * up[r, :]
        hidden[r, :] = value.astype(BF16)
        hidden_t[:, cols(i, 128)] = value.T.astype(BF16)
        return carry

    lax.fori_loop(0, slots // 128, activate, 0)

    def project(j, carry):
        row_out[:, cols(j, wcol)] = dot(hidden[...], w_all[2, j]).astype(BF16)
        return carry

    lax.fori_loop(0, nd, project, 0)
    launch(OUT)

    arrived(COT)
    arrived(COT2)
    lefts, rights = (ggp_t, gup_t, hidden_t), (row_in, row_in, cot_in)

    def part(k, j):
        return dot(lefts[k][...], rights[k][:, cols(j, wcol)]).astype(BF16)

    def both_parts(k, half):
        sib_out[k, half] = part(k, sib if half else diag)
        near_part(k, half).start()
        kept[k, half] = part(k, md if half else far)

    both_parts(2, 0)

    def backward(j, carry):
        grad_h[...] += dot(cot_in[:, cols(j, wcol)], w_all[2, j], NT)
        return carry

    lax.fori_loop(0, nd, backward, 0)

    def differentiate(i, carry):
        r = rows(i, 128)
        c = cols(i, 128)
        g = gate[r, :]
        gh = grad_h[r, :]
        s = 1.0 / (1.0 + jnp.exp(-g))
        dg = gh * up[r, :] * s * (1.0 + g * (1.0 - s))
        ggp[r, :] = dg.astype(BF16)
        ggp_t[:, c] = dg.T.astype(BF16)
        du = gh * g * s
        gup[r, :] = du.astype(BF16)
        gup_t[:, c] = du.T.astype(BF16)
        return carry

    lax.fori_loop(0, slots // 128, differentiate, 0)

    both_parts(0, 0)
    both_parts(1, 0)
    sent(COT)
    sent(COT2)

    def pull(j, carry):
        c = cols(j, wcol)
        cot_out[:, c] = (dot(ggp[...], w_all[0, j]) + dot(gup[...], w_all[1, j])).astype(BF16)
        return carry

    lax.fori_loop(0, nd, pull, 0)
    launch(GRD)
    for k in (2, 0, 1):
        near_part(k, 0).wait_recv()

        def join(i, carry):
            r = rows(i, 128)
            kept[k, 0, r, :] = (
                kept[k, 0, r, :].astype(F32) + sib_in[k, 0, r, :].astype(F32)
            ).astype(BF16)
            return carry

        lax.fori_loop(0, ff // 128, join, 0)
        far_part(k).start()
    for k in (2, 0, 1):
        both_parts(k, 1)

    arrived(OUT)

    def mix(j, carry):
        c = cols(j, wcol)
        mixture[:, c] = dot(hit_gt[...], out_in[:, c]).astype(BF16)
        return carry

    lax.fori_loop(0, nd, mix, 0)
    for k in (2, 0, 1):
        near_part(k, 1).wait_recv()
        far_part(k).wait_recv()

        def conclude(i, carry):
            r = rows(i, 128)
            total[k, r, :] = (
                kept[k, 1, r, :].astype(F32) + sib_in[k, 1, r, :].astype(F32)
            ) + far_in[k, r, :].astype(F32)
            return carry

        lax.fori_loop(0, ff // 128, conclude, 0)
        result(k).start()
    arrived(GRD)

    def home(j, carry):
        c = cols(j, wcol)
        gstream[:, c] = dot(hit_t[...], grd_in[:, c])
        return carry

    lax.fori_loop(0, nd, home, 0)

    def finish(i, carry):
        r = rows(i, 16)
        stream = resid[r, :].astype(F32) + att_in[r, :].astype(F32)
        inverse = inv_rms[r, 0:1]
        scaled = gain[...] * gstream[r, :]
        mean = jnp.sum(stream * scaled, axis=1, keepdims=True) / width
        gstream[r, :] = inverse * scaled - stream * (inverse * inverse * inverse * mean)
        return carry

    lax.fori_loop(0, steps // 16, finish, 0)

    for k in range(3):
        for half in range(2):
            near_part(k, half).wait_send()
        far_part(k).wait_send()
        result(k).wait()
        weight_to(k, 0, md).wait_send()
        weight_to(k, 1, md).wait_send()
        weight_to(k, 2, far).wait_send()
    for kind in (LEN, QKV, ATT, OUT, GRD):
        sent(kind)


def body(qkv, resid, lengths, norm_gain, expert_ids, gate_vals, w_gate, w_up, w_down, cotangent):
    series, steps, triple = qkv.shape
    width = triple // 3
    ne, nd = lax.axis_size("expert"), lax.axis_size("dp")
    _, ff, wcol = w_gate.shape
    routes = steps * expert_ids.shape[2]
    cap = 2 * routes // ne
    slots = ne * cap
    tb = steps // ne
    fits = (
        nd == 4 and ff % 128 == 0 and cap % 32 == 0 and series == 1 and w_gate.shape[0] == 1 and steps == 128 and tb % 16 == 0
        and cap % 16 == 0 and slots % 128 == 0 and wcol % 128 == 0 and expert_ids.shape[2] == 2
        and width // HEADS == 128
    )
    if not fits:
        return plain_body(
            qkv, resid, lengths, norm_gain, expert_ids, gate_vals, w_gate, w_up, w_down, cotangent
        )
    meta = jnp.concatenate([expert_ids[0].astype(F32), gate_vals[0].astype(F32)], axis=1).T
    lens = jnp.broadcast_to(lengths.astype(BF16)[:, None], (tb, 128))
    vmem = pl.BlockSpec(memory_space=pltpu.VMEM)
    hbm = pl.BlockSpec(memory_space=pl.ANY)
    dma = pltpu.SemaphoreType.DMA
    flops = 2 * slots * ff * width * 9
    mixture, gstream, *grads = pl.pallas_call(
        functools.partial(layer_kernel, ne, nd),
        out_shape=(
            jax.ShapeDtypeStruct((steps, width), BF16),
            jax.ShapeDtypeStruct((steps, width), F32),
            *[jax.ShapeDtypeStruct((ff, wcol), F32) for _ in range(3)],
        ),
        in_specs=[hbm, vmem, vmem, vmem, vmem, hbm, hbm, hbm, vmem],
        out_specs=(vmem, vmem, hbm, hbm, hbm),
        scratch_shapes=[
            pltpu.VMEM((ne * tb, 128), BF16),
            pltpu.VMEM((steps, triple), BF16),
            pltpu.VMEM((steps, width), BF16),
            pltpu.VMEM((steps, width), BF16),
            pltpu.VMEM((steps, width), BF16),
            pltpu.VMEM((steps, 128), F32),
            pltpu.VMEM((slots, steps), BF16),
            pltpu.VMEM((steps, slots), BF16),
            pltpu.VMEM((steps, slots), BF16),
            pltpu.VMEM((slots, width), BF16),
            pltpu.VMEM((slots, width), BF16),
            pltpu.VMEM((slots, width), BF16),
            pltpu.VMEM((slots, width), BF16),
            pltpu.VMEM((slots, width), BF16),
            pltpu.VMEM((slots, width), BF16),
            pltpu.VMEM((3, nd, ff, wcol), BF16),
            pltpu.VMEM((slots, ff), F32),
            pltpu.VMEM((slots, ff), F32),
            pltpu.VMEM((slots, ff), F32),
            pltpu.VMEM((slots, ff), BF16),
            pltpu.VMEM((ff, slots), BF16),
            pltpu.VMEM((slots, ff), BF16),
            pltpu.VMEM((ff, slots), BF16),
            pltpu.VMEM((slots, ff), BF16),
            pltpu.VMEM((ff, slots), BF16),
            pltpu.VMEM((3, 2, ff, wcol), BF16),
            pltpu.VMEM((3, 2, ff, wcol), BF16),
            pltpu.VMEM((3, 2, ff, wcol), BF16),
            pltpu.VMEM((3, ff, wcol), BF16),
            pltpu.VMEM((3, ff, wcol), F32),
            dma((8, ne)),
            dma((8, ne)),
            dma((3, 3)),
            dma((3, nd)),
            dma((3, 2)),
            dma((3, 2)),
            dma((3,)),
            dma((3,)),
            dma((16,)),
        ],
        compiler_params=pltpu.CompilerParams(
            collective_id=0, has_side_effects=True, vmem_limit_bytes=62 * 1024 * 1024
        ),
        cost_estimate=pl.CostEstimate(
            flops=flops, bytes_accessed=30_000_000, transcendentals=2 * slots * ff
        ),
    )(
        qkv[0], lens, resid[0], norm_gain[None, :], meta, w_gate[0], w_up[0], w_down[0],
        cotangent[0],
    )
    return (mixture[None], gstream[None], *[grad[None] for grad in grads])


def solution(mesh):
    in_specs = (
        P(("dp", "expert"), None, None),
        P(("dp", "expert"), None, None),
        P(("dp", "expert")),
        P(),
        P(("dp", "expert"), None, None),
        P(("dp", "expert"), None, None),
        P("expert", None, "dp"),
        P("expert", None, "dp"),
        P("expert", None, "dp"),
        P(("dp", "expert"), None, None),
    )
    out_specs = (
        P(("dp", "expert"), None, None),
        P(("dp", "expert"), None, None),
        P("expert", None, "dp"),
        P("expert", None, "dp"),
        P("expert", None, "dp"),
    )
    return jax.shard_map(body, mesh=mesh, in_specs=in_specs, out_specs=out_specs, check_vma=False)
```

```python
import functools
import math

import jax
import jax.numpy as jnp
from jax import lax
from jax.experimental import pallas as pl
from jax.experimental.pallas import tpu as pltpu
from jax.sharding import PartitionSpec as P

HEADS = 16
MESH = pl.DeviceIdType.MESH
F32 = jnp.float32
BF16 = jnp.bfloat16
NT = (((1,), (1,)), ((), ()))
NN = (((1,), (0,)), ((), ()))
LEN, QKV, ATT, COT, ROW, OUT, GRD, INFO = range(8)


def attend_block(queries, key_rows, value_rows, live_mask, head_size):
    scores = jnp.einsum(
        "sthc,uthc->thsu", queries, key_rows, preferred_element_type=jnp.float32
    ) / math.sqrt(head_size)
    count = queries.shape[0]
    self_pair = jnp.arange(count)[:, None] == jnp.arange(count)[None, :]
    allowed = jnp.transpose(live_mask)[:, None, None, :] | self_pair[None, None, :, :]
    masked = jnp.where(allowed, scores, -jnp.inf)
    highest = jnp.max(masked, axis=-1, keepdims=True)
    raised = jnp.exp(masked - highest)
    weights = (raised / jnp.sum(raised, axis=-1, keepdims=True)).astype(jnp.bfloat16)
    attended = jnp.einsum(
        "thsu,uthc->sthc", weights, value_rows, preferred_element_type=jnp.float32
    )
    attended = jnp.where(live_mask[:, :, None, None], attended, 0.0)
    return attended.astype(jnp.bfloat16)


def padded_rows(values):
    return jnp.concatenate([jnp.zeros((1,) + values.shape[1:], values.dtype), values], axis=0)


def plain_body(qkv, resid, lengths, norm_gain, expert_ids, gate_vals, w_gate, w_up, w_down, cotangent):
    series_here, step_count, triple = qkv.shape
    model_width = triple // 3
    head_size = model_width // HEADS
    experts_here = w_gate.shape[0]
    owners = lax.axis_size("expert")
    experts_all = experts_here * owners
    top_count = expert_ids.shape[2]
    tok_rows = series_here * step_count
    route_count = tok_rows * top_count
    capacity = 2 * route_count // experts_all
    slot_count = owners * capacity
    present = (jnp.arange(step_count)[None, :] < lengths[:, None]).astype(jnp.bfloat16)
    time_major, live_flags = (
        lax.all_to_all(qkv, "expert", split_axis=1, concat_axis=0, tiled=True),
        lax.all_to_all(present, "expert", split_axis=1, concat_axis=0, tiled=True),
    )
    group_size, time_count = live_flags.shape
    split_heads = time_major.reshape(group_size, time_count, 3, HEADS, head_size)
    attended = attend_block(
        split_heads[:, :, 0],
        split_heads[:, :, 1],
        split_heads[:, :, 2],
        live_flags > 0.5,
        head_size,
    )
    series_back = lax.all_to_all(
        attended.reshape(group_size, time_count, model_width),
        "expert",
        split_axis=0,
        concat_axis=1,
        tiled=True,
    )
    stream = resid.astype(jnp.float32) + series_back.astype(jnp.float32)
    inverse = 1.0 / jnp.sqrt(jnp.mean(stream * stream, axis=-1, keepdims=True) + 1e-05)
    normed = (stream * inverse * norm_gain).astype(jnp.bfloat16)
    route_ids = expert_ids.reshape(route_count)
    onehot = (route_ids[:, None] == jnp.arange(experts_all, dtype=jnp.int32)[None, :]).astype(
        jnp.int32
    )
    running = jnp.cumsum(onehot, axis=0, dtype=jnp.int32) - 1
    position = jnp.sum(running * onehot, axis=1, dtype=jnp.int32)
    slot_index = route_ids * capacity + position
    filled = (
        jnp.zeros((experts_all * capacity,), jnp.int32)
        .at[slot_index]
        .set(jnp.arange(1, route_count + 1, dtype=jnp.int32))
    )
    token_of = jnp.where(filled > 0, (filled - 1) // top_count + 1, 0)
    layout = (owners, experts_here, capacity, model_width)
    normed_send = padded_rows(normed.reshape(tok_rows, model_width))[token_of].reshape(layout)
    adjoint_send = padded_rows(cotangent.reshape(tok_rows, model_width))[token_of].reshape(layout)
    gate_send = padded_rows(gate_vals.reshape(route_count))[filled].reshape(
        owners, experts_here, capacity
    )
    gate_full, up_full, down_full = (
        lax.all_gather(w_gate, "dp", axis=2, tiled=True),
        lax.all_gather(w_up, "dp", axis=2, tiled=True),
        lax.all_gather(w_down, "dp", axis=2, tiled=True),
    )
    normed_recv = lax.all_to_all(normed_send, "expert", split_axis=0, concat_axis=2, tiled=True)
    x_rows = normed_recv.reshape(experts_here, slot_count, model_width)
    gate_pre = jnp.einsum("esd,efd->esf", x_rows, gate_full, preferred_element_type=jnp.float32)
    up_pre = jnp.einsum("esd,efd->esf", x_rows, up_full, preferred_element_type=jnp.float32)
    sigmoid_gate = jax.nn.sigmoid(gate_pre)
    hidden = (gate_pre * sigmoid_gate * up_pre).astype(jnp.bfloat16)
    expert_out = jnp.einsum(
        "esf,efd->esd", hidden, down_full, preferred_element_type=jnp.float32
    ).astype(jnp.bfloat16)
    back_shape = (1, experts_here, slot_count, model_width)
    out_home = lax.all_to_all(
        expert_out.reshape(back_shape), "expert", split_axis=2, concat_axis=0, tiled=True
    )
    adjoint_recv, gate_recv = (
        lax.all_to_all(adjoint_send, "expert", split_axis=0, concat_axis=2, tiled=True),
        lax.all_to_all(gate_send, "expert", split_axis=0, concat_axis=2, tiled=True),
    )
    adjoint_rows = adjoint_recv.reshape(experts_here, slot_count, model_width)
    gate_rows = gate_recv.reshape(experts_here, slot_count)
    grad_out = (
        gate_rows.astype(jnp.float32)[:, :, None] * adjoint_rows.astype(jnp.float32)
    ).astype(jnp.bfloat16)
    grad_hidden = jnp.einsum(
        "esd,efd->esf", grad_out, down_full, preferred_element_type=jnp.float32
    )
    grad_gate_pre = (
        grad_hidden * up_pre * sigmoid_gate * (1.0 + gate_pre * (1.0 - sigmoid_gate))
    ).astype(jnp.bfloat16)
    grad_up_pre = (grad_hidden * gate_pre * sigmoid_gate).astype(jnp.bfloat16)
    part_gate = jnp.einsum(
        "esf,esd->efd", grad_gate_pre, x_rows, preferred_element_type=jnp.float32
    )
    part_up = jnp.einsum("esf,esd->efd", grad_up_pre, x_rows, preferred_element_type=jnp.float32)
    part_down = jnp.einsum("esf,esd->efd", hidden, grad_out, preferred_element_type=jnp.float32)
    grad_gate, grad_up, grad_down = (
        lax.psum_scatter(
            part_gate.astype(jnp.bfloat16), "dp", scatter_dimension=2, tiled=True
        ).astype(jnp.float32),
        lax.psum_scatter(
            part_up.astype(jnp.bfloat16), "dp", scatter_dimension=2, tiled=True
        ).astype(jnp.float32),
        lax.psum_scatter(
            part_down.astype(jnp.bfloat16), "dp", scatter_dimension=2, tiled=True
        ).astype(jnp.float32),
    )
    grad_rows = jnp.einsum(
        "esf,efd->esd", grad_gate_pre, gate_full, preferred_element_type=jnp.float32
    )
    grad_rows = (
        grad_rows
        + jnp.einsum("esf,efd->esd", grad_up_pre, up_full, preferred_element_type=jnp.float32)
    ).astype(jnp.bfloat16)
    grad_home = lax.all_to_all(
        grad_rows.reshape(back_shape), "expert", split_axis=2, concat_axis=0, tiled=True
    )
    out_route = out_home.reshape(experts_all * capacity, model_width)[slot_index].reshape(
        tok_rows, top_count, model_width
    )
    grad_route = grad_home.reshape(experts_all * capacity, model_width)[slot_index].reshape(
        tok_rows, top_count, model_width
    )
    gates = gate_vals.reshape(tok_rows, top_count).astype(jnp.float32)
    mixture = jnp.sum(gates[:, :, None] * out_route.astype(jnp.float32), axis=1).astype(
        jnp.bfloat16
    )
    grad_normed = jnp.sum(grad_route.astype(jnp.float32), axis=1).reshape(
        series_here, step_count, model_width
    )
    scaled = norm_gain * grad_normed
    grad_stream = inverse * scaled - stream * inverse * inverse * inverse * jnp.mean(
        stream * scaled, axis=-1, keepdims=True
    )
    return (
        mixture.reshape(series_here, step_count, model_width),
        grad_stream,
        grad_gate,
        grad_up,
        grad_down,
    )


def dot(a, b, dims=NN):
    return lax.dot_general(a, b, dims, preferred_element_type=F32)


def layer_kernel(
    ne, nd, qkv, lens, resid, gain, info, wg, wu, wd, cot,
    mixture, gstream, g_gate, g_up, g_down,
    len_in, qkv_in, att_out, att_in, normed, inv_rms, hit, hit_g, hit_t, hit_gt,
    far_info, far_hit, far_hit_g, far_rows, far_cot,
    row_out, row_in, cot_out, cot_in, out_in, grd_in, w_all, gate, up, grad_h,
    hidden, hidden_t, ggp, ggp_t, gup, gup_t,
    sib_out, sib_in, kept, far_in, total,
    send, recv, w_send, w_recv, s_send, s_recv, f_send, f_recv, local,
):
    me = lax.axis_index("expert")
    md = lax.axis_index("dp")
    steps, width = resid.shape
    ff, wcol = wg.shape
    sib = md + 1 - 2 * lax.rem(md, 2)
    far = lax.rem(md + 2, nd)
    diag = lax.rem(sib + 2, nd)
    half = ne // 2
    base = lax.div(me, half) * half
    other = half - base
    mate = me - base + other
    tb = steps // ne
    slots = row_in.shape[0]
    cap = slots // ne
    head = width // HEADS

    def rows(block, size):
        return pl.ds(pl.multiple_of(block * size, size), size)

    def cols(block, size, base=0):
        return pl.ds(pl.multiple_of(base + block * size, 128), size)

    def remote(kind, src, dst, to, slot):
        return pltpu.make_async_remote_copy(
            src_ref=src, dst_ref=dst, send_sem=send.at[kind, to], recv_sem=recv.at[kind, slot],
            device_id={"expert": to}, device_id_type=MESH,
        )

    def ends(kind):
        if kind == LEN:
            return lens, len_in, None, tb
        if kind == QKV:
            return qkv, qkv_in, tb, tb
        if kind == ATT:
            return att_out, att_in, tb, tb
        if kind == COT:
            return cot_out, cot_in, cap, cap
        if kind == ROW:
            return row_out, row_in, cap, cap
        if kind == OUT:
            return row_out, out_in, cap, cap
        return cot_out, grd_in, cap, cap

    def copy_to(kind, to, slot):
        src, dst, from_rows, to_rows = ends(kind)
        part = src if from_rows is None else src.at[rows(to, from_rows)]
        return remote(kind, part, dst.at[rows(slot, to_rows)], to, slot)

    def own(kind):
        src, dst, from_rows, to_rows = ends(kind)
        part = src if from_rows is None else src.at[rows(me, from_rows)]
        return pltpu.make_async_copy(part, dst.at[rows(me, to_rows)], local.at[kind])

    def each(count, base, act):
        def step(i, carry):
            act(lax.rem(base + i, count))
            return carry

        lax.fori_loop(1, count, step, 0)

    def all_peers(act):
        def step(i, carry):
            d = ne - i
            side = lax.rem(lax.div(me, 4) + lax.div(d, 4), 2)
            line = lax.rem(lax.rem(lax.div(me, 2), 2) + lax.rem(lax.div(d, 2), 2), 2)
            edge = lax.rem(lax.rem(me, 2) + lax.rem(d, 2), 2)
            act(4 * side + 2 * line + edge)
            return carry

        lax.fori_loop(1, ne, step, 0)

    def near_peers(act):
        def step(i, carry):
            act(base + lax.rem(me - base + i, half))
            return carry

        lax.fori_loop(1, half, step, 0)

    def across(kind):
        src, dst = {INFO: (info, far_info), ROW: (normed, far_rows), COT: (cot, far_cot)}[kind]
        return remote(kind, src, dst, mate, me)

    def crossed(kind):
        src, dst = {INFO: (info, far_info), ROW: (normed, far_rows), COT: (cot, far_cot)}[kind]
        remote(kind, src, dst, mate, mate).wait_recv()

    def relay(kind, p, slot):
        src, dst, size, _ = ends(kind)
        return pltpu.make_async_remote_copy(
            src_ref=src.at[rows(p - base + other, size)], dst_ref=dst.at[rows(slot, size)],
            send_sem=send.at[kind, p - base + other], recv_sem=recv.at[kind, slot],
            device_id={"expert": p}, device_id_type=MESH,
        )

    def relay_own(kind):
        src, dst, size, _ = ends(kind)
        return pltpu.make_async_copy(
            src.at[rows(mate, size)], dst.at[rows(mate, size)], local.at[kind + 11]
        )

    def launch_near(kind):
        near_peers(lambda p: copy_to(kind, p, me).start())
        own(kind).start()

    def launch_relay(kind):
        near_peers(lambda p: relay(kind, p, mate).start())
        relay_own(kind).start()

    def gathered(kind):
        near_peers(lambda p: copy_to(kind, p, p).wait_recv())
        near_peers(lambda p: relay(kind, p, p - base + other).wait_recv())
        own(kind).wait()
        relay_own(kind).wait()

    def passed(kind):
        near_peers(lambda p: copy_to(kind, p, me).wait_send())
        near_peers(lambda p: relay(kind, p, mate).wait_send())
        across(kind).wait_send()

    def launch(kind):
        all_peers(lambda p: copy_to(kind, p, me).start())
        own(kind).start()

    def arrived(kind):
        all_peers(lambda p: copy_to(kind, p, p).wait_recv())
        own(kind).wait()

    def sent(kind):
        all_peers(lambda p: copy_to(kind, p, me).wait_send())

    shards = (wg, wu, wd)

    def weight_to(k, way, slot):
        src = w_all.at[k, slot] if way == 2 else shards[k]
        return pltpu.make_async_remote_copy(
            src_ref=src, dst_ref=w_all.at[k, slot], send_sem=w_send.at[k, way],
            recv_sem=w_recv.at[k, slot], device_id={"dp": far if way == 1 else sib},
            device_id_type=MESH,
        )

    def weight_own(k):
        return pltpu.make_async_copy(shards[k], w_all.at[k, md], local.at[8 + k])

    def near_part(k, half):
        return pltpu.make_async_remote_copy(
            src_ref=sib_out.at[k, half], dst_ref=sib_in.at[k, half], send_sem=s_send.at[k, half],
            recv_sem=s_recv.at[k, half], device_id={"dp": sib}, device_id_type=MESH,
        )

    def far_part(k):
        return pltpu.make_async_remote_copy(
            src_ref=kept.at[k, 0], dst_ref=far_in.at[k], send_sem=f_send.at[k],
            recv_sem=f_recv.at[k], device_id={"dp": far}, device_id_type=MESH,
        )

    def result(k):
        return pltpu.make_async_copy(total.at[k], (g_gate, g_up, g_down)[k], local.at[18 + k])

    barrier = pltpu.get_barrier_semaphore()
    each(ne, me, lambda p: pl.semaphore_signal(
        barrier, inc=1, device_id={"expert": p}, device_id_type=MESH))
    for p in (sib, far):
        pl.semaphore_signal(barrier, inc=1, device_id={"dp": p}, device_id_type=MESH)
    pl.semaphore_wait(barrier, ne + 1)

    across(INFO).start()
    launch(LEN)
    launch(QKV)
    for k in range(3):
        weight_to(k, 1, md).start()
        weight_to(k, 0, md).start()
        weight_own(k).start()

    row_id = lax.broadcasted_iota(jnp.int32, (steps, steps), 0)
    col_id = lax.broadcasted_iota(jnp.int32, (steps, steps), 1)
    before = jnp.where(row_id < col_id, 1.0, 0.0).astype(BF16)
    slot = lax.broadcasted_iota(jnp.int32, (cap, steps), 0).astype(F32)
    per = 128 // cap

    def routing(named_by, lowest, count, store):
        known = named_by[...].astype(F32)
        expert = (lax.broadcasted_iota(jnp.int32, (16, steps), 0) + lowest).astype(F32)
        first, second = known[0:1, :], known[1:2, :]
        named = jnp.where(expert == first, 1.0, 0.0) + jnp.where(expert == second, 1.0, 0.0)
        place = jnp.where(named > 0.5, dot(named.astype(BF16), before), -1.0)
        value = jnp.where(expert == first, known[2:3, :], known[3:4, :])
        for e in range(0, count, per):
            ones, weighted = [], []
            for i in range(e, e + per):
                same = place[i : i + 1, :] == slot
                ones.append(jnp.where(same, 1.0, 0.0))
                weighted.append(jnp.where(same, value[i : i + 1, :], 0.0))
            store(
                slice(e * cap, (e + per) * cap),
                jnp.concatenate(ones, axis=0),
                jnp.concatenate(weighted, axis=0),
            )

    def store_own(piece, one, scaled):
        hit[piece, :] = one.astype(BF16)
        hit_g[piece, :] = scaled.astype(BF16)
        hit_t[:, piece] = one.T.astype(BF16)
        hit_gt[:, piece] = scaled.T.astype(BF16)

    def store_far(piece, one, scaled):
        far_hit[piece, :] = one.astype(BF16)
        far_hit_g[piece, :] = scaled.astype(BF16)

    mine = pl.ds(pl.multiple_of(base * cap, half * cap), half * cap)
    theirs = pl.ds(pl.multiple_of(other * cap, half * cap), half * cap)

    def cut(where, choose, source, target):
        def step(j, carry):
            c = cols(j, wcol)
            target[where, c] = dot(choose, source[:, c]).astype(BF16)
            return carry

        lax.fori_loop(0, nd, step, 0)

    routing(info, 0, ne, store_own)
    crossed(INFO)
    routing(far_info, base, half, store_far)
    cut(mine, hit_g[mine, :], cot, cot_out)

    arrived(LEN)
    arrived(QKV)
    across(COT).start()
    row_len = len_in[...].astype(F32)
    col_len = row_len.T
    r_id = lax.broadcasted_iota(jnp.int32, (steps, steps), 0)
    c_id = lax.broadcasted_iota(jnp.int32, (steps, steps), 1)
    r_time, c_time = lax.rem(r_id, tb), lax.rem(c_id, tb)
    start = me * tb
    seen = ((c_time + start).astype(F32) < col_len) | (r_id == c_id)
    bias = jnp.where((r_time == c_time) & seen, 0.0, -jnp.inf)
    live = jnp.where((r_time + start).astype(F32) < row_len, 1.0, 0.0)

    def attend(h, carry):
        q = qkv_in[:, cols(h, head)]
        k = qkv_in[:, cols(h, head, width)]
        v = qkv_in[:, cols(h, head, 2 * width)]
        scores = dot(q, k, NT) / math.sqrt(head) + bias
        raised = jnp.exp(scores - jnp.max(scores, axis=1, keepdims=True))
        weights = (raised / jnp.sum(raised, axis=1, keepdims=True)).astype(BF16)
        att_out[:, cols(h, head)] = (dot(weights, v) * live).astype(BF16)
        return carry

    lax.fori_loop(0, HEADS, attend, 0)
    launch(ATT)
    arrived(ATT)

    def norm(i, carry):
        r = rows(i, 16)
        stream = resid[r, :].astype(F32) + att_in[r, :].astype(F32)
        mean = jnp.sum(stream * stream, axis=1, keepdims=True) / width
        inverse = 1.0 / jnp.sqrt(mean + 1e-05)
        inv_rms[r, :] = jnp.broadcast_to(inverse, (16, 128))
        normed[r, :] = (stream * inverse * gain[...]).astype(BF16)
        return carry

    lax.fori_loop(0, steps // 16, norm, 0)

    across(ROW).start()
    cut(mine, hit[mine, :], normed, row_out)
    launch_near(ROW)
    crossed(COT)
    cut(theirs, far_hit_g[...], far_cot, cot_out)
    crossed(ROW)
    cut(theirs, far_hit[...], far_rows, row_out)
    launch_relay(ROW)
    launch_relay(COT)
    launch_near(COT)
    for k in range(3):
        weight_to(k, 1, far).wait_recv()
        weight_to(k, 2, far).start()
    for k in range(3):
        weight_to(k, 0, sib).wait_recv()
        weight_to(k, 2, diag).wait_recv()
        weight_own(k).wait()
    gathered(ROW)

    gate[...] = jnp.zeros_like(gate)
    up[...] = jnp.zeros_like(up)
    grad_h[...] = jnp.zeros_like(grad_h)

    def forward(j, carry):
        x = row_in[:, cols(j, wcol)]
        gate[...] += dot(x, w_all[0, j], NT)
        up[...] += dot(x, w_all[1, j], NT)
        return carry

    lax.fori_loop(0, nd, forward, 0)

    def activate(i, carry):
        r = rows(i, 128)
        g = gate[r, :]
        value = g * (1.0 / (1.0 + jnp.exp(-g))) * up[r, :]
        hidden[r, :] = value.astype(BF16)
        hidden_t[:, cols(i, 128)] = value.T.astype(BF16)
        return carry

    lax.fori_loop(0, slots // 128, activate, 0)

    passed(ROW)

    def project(j, carry):
        row_out[:, cols(j, wcol)] = dot(hidden[...], w_all[2, j]).astype(BF16)
        return carry

    lax.fori_loop(0, nd, project, 0)
    launch(OUT)

    gathered(COT)
    lefts, rights = (ggp_t, gup_t, hidden_t), (row_in, row_in, cot_in)

    def part(k, j):
        return dot(lefts[k][...], rights[k][:, cols(j, wcol)]).astype(BF16)

    def both_parts(k, half):
        sib_out[k, half] = part(k, sib if half else diag)
        near_part(k, half).start()
        kept[k, half] = part(k, md if half else far)

    both_parts(2, 0)

    def backward(j, carry):
        grad_h[...] += dot(cot_in[:, cols(j, wcol)], w_all[2, j], NT)
        return carry

    lax.fori_loop(0, nd, backward, 0)

    def differentiate(i, carry):
        r = rows(i, 128)
        c = cols(i, 128)
        g = gate[r, :]
        gh = grad_h[r, :]
        s = 1.0 / (1.0 + jnp.exp(-g))
        dg = gh * up[r, :] * s * (1.0 + g * (1.0 - s))
        ggp[r, :] = dg.astype(BF16)
        ggp_t[:, c] = dg.T.astype(BF16)
        du = gh * g * s
        gup[r, :] = du.astype(BF16)
        gup_t[:, c] = du.T.astype(BF16)
        return carry

    lax.fori_loop(0, slots // 128, differentiate, 0)

    both_parts(0, 0)
    both_parts(1, 0)
    passed(COT)

    def pull(j, carry):
        c = cols(j, wcol)
        cot_out[:, c] = (dot(ggp[...], w_all[0, j]) + dot(gup[...], w_all[1, j])).astype(BF16)
        return carry

    lax.fori_loop(0, nd, pull, 0)
    launch(GRD)
    for k in (2, 0, 1):
        near_part(k, 0).wait_recv()

        def join(i, carry):
            r = rows(i, 128)
            kept[k, 0, r, :] = (
                kept[k, 0, r, :].astype(F32) + sib_in[k, 0, r, :].astype(F32)
            ).astype(BF16)
            return carry

        lax.fori_loop(0, ff // 128, join, 0)
        far_part(k).start()
    for k in (2, 0, 1):
        both_parts(k, 1)

    arrived(OUT)

    def mix(j, carry):
        c = cols(j, wcol)
        mixture[:, c] = dot(hit_gt[...], out_in[:, c]).astype(BF16)
        return carry

    lax.fori_loop(0, nd, mix, 0)
    for k in (2, 0, 1):
        near_part(k, 1).wait_recv()
        far_part(k).wait_recv()

        def conclude(i, carry):
            r = rows(i, 128)
            total[k, r, :] = (
                kept[k, 1, r, :].astype(F32) + sib_in[k, 1, r, :].astype(F32)
            ) + far_in[k, r, :].astype(F32)
            return carry

        lax.fori_loop(0, ff // 128, conclude, 0)
        result(k).start()
    arrived(GRD)

    def home(j, carry):
        c = cols(j, wcol)
        gstream[:, c] = dot(hit_t[...], grd_in[:, c])
        return carry

    lax.fori_loop(0, nd, home, 0)

    def finish(i, carry):
        r = rows(i, 16)
        stream = resid[r, :].astype(F32) + att_in[r, :].astype(F32)
        inverse = inv_rms[r, 0:1]
        scaled = gain[...] * gstream[r, :]
        mean = jnp.sum(stream * scaled, axis=1, keepdims=True) / width
        gstream[r, :] = inverse * scaled - stream * (inverse * inverse * inverse * mean)
        return carry

    lax.fori_loop(0, steps // 16, finish, 0)

    for k in range(3):
        for half in range(2):
            near_part(k, half).wait_send()
        far_part(k).wait_send()
        result(k).wait()
        weight_to(k, 0, md).wait_send()
        weight_to(k, 1, md).wait_send()
        weight_to(k, 2, far).wait_send()
    for kind in (LEN, QKV, ATT, OUT, GRD):
        sent(kind)
    across(INFO).wait_send()


def body(qkv, resid, lengths, norm_gain, expert_ids, gate_vals, w_gate, w_up, w_down, cotangent):
    series, steps, triple = qkv.shape
    width = triple // 3
    ne, nd = lax.axis_size("expert"), lax.axis_size("dp")
    _, ff, wcol = w_gate.shape
    routes = steps * expert_ids.shape[2]
    cap = 2 * routes // ne
    slots = ne * cap
    tb = steps // ne
    fits = (
        nd == 4 and ne == 8 and ff % 128 == 0 and cap % 32 == 0 and series == 1 and w_gate.shape[0] == 1 and steps == 128 and tb % 16 == 0
        and cap % 16 == 0 and slots % 128 == 0 and wcol % 128 == 0 and expert_ids.shape[2] == 2
        and width // HEADS == 128
    )
    if not fits:
        return plain_body(
            qkv, resid, lengths, norm_gain, expert_ids, gate_vals, w_gate, w_up, w_down, cotangent
        )
    routed = jnp.concatenate([expert_ids[0].astype(BF16), gate_vals[0]], axis=1)
    info = jnp.pad(routed, ((0, 0), (0, 12))).T
    lens = jnp.broadcast_to(lengths.astype(BF16)[:, None], (tb, 128))
    vmem = pl.BlockSpec(memory_space=pltpu.VMEM)
    hbm = pl.BlockSpec(memory_space=pl.ANY)
    dma = pltpu.SemaphoreType.DMA
    flops = 2 * slots * ff * width * 9
    mixture, gstream, *grads = pl.pallas_call(
        functools.partial(layer_kernel, ne, nd),
        out_shape=(
            jax.ShapeDtypeStruct((steps, width), BF16),
            jax.ShapeDtypeStruct((steps, width), F32),
            *[jax.ShapeDtypeStruct((ff, wcol), F32) for _ in range(3)],
        ),
        in_specs=[hbm, vmem, vmem, vmem, vmem, hbm, hbm, hbm, vmem],
        out_specs=(vmem, vmem, hbm, hbm, hbm),
        scratch_shapes=[
            pltpu.VMEM((ne * tb, 128), BF16),
            pltpu.VMEM((steps, triple), BF16),
            pltpu.VMEM((steps, width), BF16),
            pltpu.VMEM((steps, width), BF16),
            pltpu.VMEM((steps, width), BF16),
            pltpu.VMEM((steps, 128), F32),
            pltpu.VMEM((slots, steps), BF16),
            pltpu.VMEM((slots, steps), BF16),
            pltpu.VMEM((steps, slots), BF16),
            pltpu.VMEM((steps, slots), BF16),
            pltpu.VMEM((16, steps), BF16),
            pltpu.VMEM((slots // 2, steps), BF16),
            pltpu.VMEM((slots // 2, steps), BF16),
            pltpu.VMEM((steps, width), BF16),
            pltpu.VMEM((steps, width), BF16),
            pltpu.VMEM((slots, width), BF16),
            pltpu.VMEM((slots, width), BF16),
            pltpu.VMEM((slots, width), BF16),
            pltpu.VMEM((slots, width), BF16),
            pltpu.VMEM((slots, width), BF16),
            pltpu.VMEM((slots, width), BF16),
            pltpu.VMEM((3, nd, ff, wcol), BF16),
            pltpu.VMEM((slots, ff), F32),
            pltpu.VMEM((slots, ff), F32),
            pltpu.VMEM((slots, ff), F32),
            pltpu.VMEM((slots, ff), BF16),
            pltpu.VMEM((ff, slots), BF16),
            pltpu.VMEM((slots, ff), BF16),
            pltpu.VMEM((ff, slots), BF16),
            pltpu.VMEM((slots, ff), BF16),
            pltpu.VMEM((ff, slots), BF16),
            pltpu.VMEM((3, 2, ff, wcol), BF16),
            pltpu.VMEM((3, 2, ff, wcol), BF16),
            pltpu.VMEM((3, 2, ff, wcol), BF16),
            pltpu.VMEM((3, ff, wcol), BF16),
            pltpu.VMEM((3, ff, wcol), F32),
            dma((8, ne)),
            dma((8, ne)),
            dma((3, 3)),
            dma((3, nd)),
            dma((3, 2)),
            dma((3, 2)),
            dma((3,)),
            dma((3,)),
            dma((24,)),
        ],
        compiler_params=pltpu.CompilerParams(
            collective_id=0, has_side_effects=True, vmem_limit_bytes=62 * 1024 * 1024
        ),
        cost_estimate=pl.CostEstimate(
            flops=flops, bytes_accessed=30_000_000, transcendentals=2 * slots * ff
        ),
    )(
        qkv[0], lens, resid[0], norm_gain[None, :], info, w_gate[0], w_up[0], w_down[0],
        cotangent[0],
    )
    return (mixture[None], gstream[None], *[grad[None] for grad in grads])


def solution(mesh):
    in_specs = (
        P(("dp", "expert"), None, None),
        P(("dp", "expert"), None, None),
        P(("dp", "expert")),
        P(),
        P(("dp", "expert"), None, None),
        P(("dp", "expert"), None, None),
        P("expert", None, "dp"),
        P("expert", None, "dp"),
        P("expert", None, "dp"),
        P(("dp", "expert"), None, None),
    )
    out_specs = (
        P(("dp", "expert"), None, None),
        P(("dp", "expert"), None, None),
        P("expert", None, "dp"),
        P("expert", None, "dp"),
        P("expert", None, "dp"),
    )
    return jax.shard_map(body, mesh=mesh, in_specs=in_specs, out_specs=out_specs, check_vma=False)
```
